32 devices in a mesh: groups: 2 (over y), pool: 4 (over x, core), tp: 4 (over z).
Axes of the slice: x: 2, y: 2, z: 4, core: 2. Of those that a mesh axis runs over, the one named last changes fastest.
Arguments:
- queries: bfloat16 [4, 512, 8192], P('groups', 'pool', 'tp'), parts along dimension 0, may hold values from -4.5 to 4.5
- span_kv: bfloat16 [4, 512, 8, 256], P('groups', 'pool'), parts along dimension 0, may hold values from -4.5 to 4.5
- prefix_pool: bfloat16 [192, 128, 8, 256], P(('groups', 'pool'), 'tp'), parts along dimension 0, may hold values from -4.5 to 4.5
- hit_blocks: int32 [4, 24], P('groups'), parts along dimension 0, may hold values from 0 to 95, as said below
- prefix_len: int32 [4], P('groups'), parts along dimension 0, may hold values from 12 to 24, as said below
- dest_blocks: int32 [4, 4], P('groups'), parts along dimension 0, may hold values from 0 to 95, as said below
- out_w: bfloat16 [8192, 8192], P('tp'), may hold values from -0.375 to 0.375
- residual: bfloat16 [4, 512, 8192], P('groups', 'pool', 'tp'), parts along dimension 0, may hold values from -3 to 3
- norm_gain: bfloat16 [8192], P('tp'), may hold values from 0.5 to 1.5
Outputs:
- hidden: bfloat16 [4, 512, 8192], P('groups', 'pool', 'tp'), parts along dimension 0
- normed: bfloat16 [4, 512, 8192], P('groups', 'pool', 'tp'), parts along dimension 0
- new_pool: bfloat16 [192, 128, 8, 256], P(('groups', 'pool'), 'tp'), parts along dimension 0
The draws below stay inside these ranges and needn't reach their ends.
There are 2 independent parts, one for each index of `groups`. The reference program is written for one: setup_inputs(seed, part) draws one part's arguments, and reference() takes and returns one part's arrays. A program takes and returns all parts, laid end to end along the dimension named above; an argument that names none is the same for every part. Nothing has to cross between parts.
Inputs may be any that keep to these rules, and one draw needn't show every extreme that they name: Block ids in hit_blocks are all distinct. Row j's first prefix_len[j] entries are prompt j's prefix blocks in order; later entries are unused. Block b lies on pool index b // 24. Over both prompts at most 12 used entries lie on one pool index, and some pool index holds exactly 12. `prefix_len`: one prompt has exactly 24 prefix blocks. `dest_blocks`: all distinct, and none appears in hit_blocks.
All inputs are finite; a program needn't handle non-finite values.
Results may differ from the reference program's by a relative error of at most 0.008.
Values may be sent and summed in bfloat16 or wider, within the bound.
No kernel may reach another device: no remote copies, remote signals or barrier semaphores. Data moves between devices by JAX's collectives and lax.ppermute only.
A program may use at most 192 MiB of HBM per device.

```python
import math
import jax
import jax.numpy as jnp
from jax import lax

D = 8192
QH = 64
KVH = 8
HD = 128
BLOCK = 128
PROMPTS = 2
MAXB = 24
MOST = 12
BLK_DEV = 24
SPAN = 512
SPAN_BLOCKS = 4
POOL_BLOCKS = 96


def shuffle_slots(stream):
    return jax.random.permutation(stream, BLK_DEV)


def block_layout(key):
    key = jax.random.fold_in(key, 11)
    streams = jax.random.split(key, 6)
    holders = POOL_BLOCKS // BLK_DEV
    longest = jax.random.randint(streams[0], (), 0, PROMPTS)
    lengths = jax.random.randint(streams[1], (PROMPTS,), MAXB // 2, MAXB + 1)
    lengths = jnp.where(jnp.arange(PROMPTS) == longest, MAXB, lengths).astype(jnp.int32)
    busiest = jax.random.randint(streams[2], (), 0, holders)
    others = jax.random.permutation(streams[3], holders - 1)
    entry = jnp.arange(PROMPTS * MAXB)
    prompt_of = entry // MAXB
    position = entry % MAXB
    crowded = (prompt_of == longest) & (position < MOST)
    ordinal = jnp.cumsum(1 - crowded.astype(jnp.int32)) - 1
    holder = jnp.where(crowded, busiest, (busiest + 1 + others[ordinal % (holders - 1)]) % holders)
    onehot = (holder[:, None] == jnp.arange(holders)[None, :]).astype(jnp.int32)
    slot_rank = jnp.sum((jnp.cumsum(onehot, axis=0) - 1) * onehot, axis=1)
    write_no = jnp.arange(PROMPTS * SPAN_BLOCKS)
    write_perm = jax.random.permutation(streams[4], holders)
    write_holder = write_perm[write_no % holders]
    write_rank = BLK_DEV - 1 - write_no // holders
    slot_perm = jax.vmap(shuffle_slots)(jax.random.split(streams[5], holders))
    hit_ids = holder * BLK_DEV + slot_perm[holder, slot_rank]
    dest_ids = write_holder * BLK_DEV + slot_perm[write_holder, write_rank]
    return (hit_ids.reshape(PROMPTS, MAXB).astype(jnp.int32), lengths, dest_ids.reshape(PROMPTS, SPAN_BLOCKS).astype(jnp.int32))


def draw_hit_blocks(key, part):
    return block_layout(key)[0]


def draw_prefix_len(key, part):
    return block_layout(key)[1]


def draw_dest_blocks(key, part):
    return block_layout(key)[2]


def draw_queries(key, part):
    key = jax.random.fold_in(key, 1)
    values = jnp.clip(2.0 * jax.random.normal(key, (PROMPTS, SPAN, QH, HD), jnp.float32), -4.5, 4.5)
    return values.reshape(PROMPTS, SPAN, QH * HD).astype(jnp.bfloat16)


def draw_span_kv(key, part):
    key = jax.random.fold_in(key, 2)
    values = jnp.clip(jax.random.normal(key, (PROMPTS, SPAN, KVH, 2 * HD), jnp.float32), -4.5, 4.5)
    return values.astype(jnp.bfloat16)


def raised(entries, stream_key, source, target, shards_of, factor):
    def block_of(axis_at):
        return (jnp.arange(entries.shape[axis_at]) // (entries.shape[axis_at] // shards_of)).reshape((-1,) + (1,) * (entries.ndim - 1 - axis_at))

    near = jax.random.permutation(stream_key, shards_of)[block_of(target)]
    other_side = (block_of(target) + shards_of // 2) % shards_of
    return jnp.where((block_of(source) == near) | (block_of(source) == other_side), factor * entries, entries)


def levels(stream_key, dims, cuts, low, top_value):
    factor_of = 1.0
    for dim, shards_of in cuts:
        draws = jax.random.uniform(jax.random.fold_in(jax.random.fold_in(stream_key, 6), dim), (shards_of,), jnp.float32, low / len(cuts), top_value / len(cuts))
        factor_of = factor_of * jnp.repeat(jnp.exp(draws), dims[dim] // shards_of).reshape((-1,) + (1,) * (len(dims) - 1 - dim))
    return factor_of


def noise(key, dims, width, limit, pieces=(), dtype=jnp.bfloat16):
    array = width * jax.random.normal(key, dims, jnp.float32)
    if pieces:
        array = array * levels(key, dims, pieces, -0.22, 0.18)
    return jnp.clip(array, -limit, limit).astype(dtype)


def noise_with(key, dims, spread, reach, pieces, heavy, kind=jnp.bfloat16):
    drawn = spread * jax.random.normal(key, dims, jnp.float32)
    if pieces:
        drawn = drawn * levels(key, dims, pieces, -0.22, 0.18)
    return jnp.clip(raised(drawn, jax.random.fold_in(key, 3), *heavy), -reach, reach).astype(kind)


def setup_inputs(seed: int = 0, part: int = 0) -> dict:
    key_list = jax.random.split(jax.random.key(seed), 10)
    own_keys = jax.random.split(jax.random.fold_in(key_list[9], part), 10)
    queries = draw_queries(jax.random.fold_in(jax.random.fold_in(key_list[9], part), 71), part)
    span_kv = draw_span_kv(jax.random.fold_in(jax.random.fold_in(key_list[9], part), 71), part)
    prefix_pool = noise(own_keys[2], (POOL_BLOCKS, BLOCK, KVH, 2 * HD), 1.0, 4.5, ((0, 4), (1, 4)))
    hit_blocks = draw_hit_blocks(jax.random.fold_in(jax.random.fold_in(key_list[9], part), 71), part)
    prefix_len = draw_prefix_len(jax.random.fold_in(jax.random.fold_in(key_list[9], part), 71), part)
    dest_blocks = draw_dest_blocks(jax.random.fold_in(jax.random.fold_in(key_list[9], part), 71), part)
    out_w = noise_with(key_list[6], (QH * HD, D), (QH * HD // 16) ** -0.5, 0.375, ((0, 4),), (0, 1, 4, 2.0))
    residual = noise(own_keys[7], (PROMPTS, SPAN, D), 0.5, 3.0, ((1, 4), (2, 4)))
    norm_gain = jnp.clip(1.0 + 0.1 * jax.random.normal(key_list[8], (D,), jnp.float32), 0.5, 1.5).astype(jnp.bfloat16)
    return {"queries": queries, "span_kv": span_kv, "prefix_pool": prefix_pool, "hit_blocks": hit_blocks, "prefix_len": prefix_len, "dest_blocks": dest_blocks, "out_w": out_w, "residual": residual, "norm_gain": norm_gain}


def reference(queries, span_kv, prefix_pool, hit_blocks, prefix_len, dest_blocks, out_w, residual, norm_gain):
    sharing = QH // KVH
    score_scale = 1.0 / math.sqrt(HD)
    prefix_rows = MAXB * BLOCK
    attended_list = []
    for prompt in range(PROMPTS):
        fetched = jnp.take(prefix_pool, hit_blocks[prompt], axis=0).reshape(prefix_rows, KVH, 2 * HD)
        joined = jnp.concatenate([fetched, span_kv[prompt]], axis=0).astype(jnp.float32)
        key_part = joined[..., :HD]
        value_part = joined[..., HD:]
        key_index = jnp.arange(prefix_rows + SPAN)
        prefix_live = key_index < prefix_len[prompt] * BLOCK
        query_grid = queries[prompt].astype(jnp.float32).reshape(SPAN // BLOCK, BLOCK, KVH, sharing, HD)

        def one_block(inputs):
            rows, block_number = inputs
            query_pos = block_number * BLOCK + jnp.arange(BLOCK)
            visible = jnp.where(key_index[None, :] < prefix_rows, prefix_live[None, :], key_index[None, :] - prefix_rows <= query_pos[:, None])
            scores = jnp.einsum('ikgd,nkd->ikgn', rows, key_part) * score_scale
            scores = jnp.where(visible[:, None, None, :], scores, -jnp.inf)
            peak = lax.optimization_barrier(jnp.max(scores, axis=-1, keepdims=True))
            weights = jnp.exp(scores - peak)
            summed = jnp.einsum('ikgn,nkd->ikgd', weights, value_part)
            return summed / lax.optimization_barrier(jnp.sum(weights, axis=-1))[..., None]
        blocks_out = lax.map(one_block, (query_grid, jnp.arange(SPAN // BLOCK)))
        attended_list.append(blocks_out.astype(jnp.bfloat16).reshape(SPAN, QH * HD))
    attended = jnp.concatenate(attended_list, axis=0)
    projected = jnp.dot(attended, out_w, preferred_element_type=jnp.float32)
    hidden = (residual.reshape(PROMPTS * SPAN, D).astype(jnp.float32) + projected).astype(jnp.bfloat16)
    hidden = lax.optimization_barrier(hidden)
    widened = hidden.astype(jnp.float32)
    mean_square = lax.optimization_barrier(jnp.mean(widened * widened, axis=1, keepdims=True))
    normed = (widened * lax.rsqrt(mean_square + 1e-05) * norm_gain.astype(jnp.float32)[None, :]).astype(jnp.bfloat16)
    written = span_kv.reshape(PROMPTS * SPAN_BLOCKS, BLOCK, KVH, 2 * HD)
    new_pool = prefix_pool.at[dest_blocks.reshape(-1)].set(written)
    return (hidden.reshape(PROMPTS, SPAN, D), normed.reshape(PROMPTS, SPAN, D), new_pool)
```

```python
import functools
import math

import jax
import jax.numpy as jnp
from jax import lax
from jax.experimental import pallas as pl
from jax.experimental.pallas import tpu as pltpu
from jax.sharding import PartitionSpec as P

QH = 64
KVH = 8
HD = 128
MAXB = 24
MOST = 12

epsilon = 1e-05
lowest = -1e30
exponent_scale = math.log2(math.e) / math.sqrt(HD)
VMEM_LIMIT = 56 * 1024 * 1024

SMEM = functools.partial(pl.BlockSpec, memory_space=pltpu.SMEM)
VMEM = functools.partial(pl.BlockSpec, memory_space=pltpu.VMEM)
ANY = functools.partial(pl.BlockSpec, memory_space=pl.ANY)


def holder_of(relative, pool_index, pool_count):
    chips = pool_count // 2
    chip = lax.rem(pool_index // 2 + chips - relative // 2, chips)
    core = lax.rem(lax.rem(pool_index, 2) + relative % 2, 2)
    return chip * 2 + core


def prepare_kernel(
    tp_count, pool_count, heads_dev, hit, lens, place, pool, span, *refs
):
    counts = refs[0]
    sends = refs[1 : 1 + tp_count]
    span_out = refs[1 + tp_count]
    own_slots, held, wide, sems = refs[2 + tp_count :]
    prompts, rows_dev = span.shape[:2]
    slots_dev, block_rows = pool.shape[:2]
    kv_dev = span_out.shape[0]
    sharing = QH // KVH
    pool_index = place[0]
    tp_index = place[1]
    for slot in range(MOST):
        own_slots[slot] = 0
    own_slots[MOST] = 0
    for prompt in range(prompts):
        for relative in range(pool_count):
            counts[prompt, relative] = 0

        def entry(position, carry, prompt=prompt):
            block = hit[prompt, position]
            holder = block // slots_dev
            chips = pool_count // 2
            chip_away = lax.rem(pool_index // 2 + chips - holder // 2, chips)
            core_away = lax.rem(lax.rem(pool_index, 2) + lax.rem(holder, 2), 2)
            relative = chip_away * 2 + core_away
            counts[prompt, relative] = counts[prompt, relative] + 1

            @pl.when(holder == pool_index)
            def _():
                rank = own_slots[MOST]
                own_slots[rank] = block - holder * slots_dev
                own_slots[MOST] = rank + 1

            return carry

        lax.fori_loop(0, lens[prompt], entry, 0)
    copies = []
    for slot in range(MOST):
        copy = pltpu.make_async_copy(pool.at[own_slots[slot]], held.at[slot], sems.at[slot])
        copy.start()
        copies.append(copy)

    def first_head(shift):
        device = lax.rem(tp_index + shift, tp_count)
        return device * heads_dev // sharing

    def spread(block, rows):
        for half in range(2):
            wide[half, pl.ds(0, rows * KVH), :] = (
                block[:, :, half * HD : (half + 1) * HD].astype(jnp.float32).reshape(rows * KVH, HD)
            )

    def one_head(head, rows):
        here = pl.ds(head, rows, stride=KVH)
        return jnp.concatenate([wide[half, here, :] for half in range(2)], axis=1).astype(
            jnp.bfloat16
        )

    for prompt in range(prompts):
        spread(span[prompt], rows_dev)
        for head in range(kv_dev):
            span_out[head, prompt] = one_head(first_head(0) + head, rows_dev)
    for slot in range(MOST):
        copies[slot].wait()
        spread(held[slot], block_rows)
        for shift in range(tp_count):
            for head in range(kv_dev):
                sends[shift][slot, head] = one_head(first_head(shift) + head, block_rows)


def prepare(tp_count, pool_count, heads_dev, kv_dev, hit, lens, place, pool, span):
    prompts, rows_dev = span.shape[:2]
    block_rows = pool.shape[1]
    send = jax.ShapeDtypeStruct((MOST, kv_dev, block_rows, 2 * HD), jnp.bfloat16)
    outs = pl.pallas_call(
        functools.partial(prepare_kernel, tp_count, pool_count, heads_dev),
        out_shape=[jax.ShapeDtypeStruct((prompts, pool_count), jnp.int32)]
        + [send] * tp_count
        + [jax.ShapeDtypeStruct((kv_dev, prompts, rows_dev, 2 * HD), jnp.bfloat16)],
        in_specs=[SMEM(), SMEM(), SMEM(), ANY(), VMEM()],
        out_specs=[SMEM()] + [VMEM()] * (tp_count + 1),
        scratch_shapes=[
            pltpu.SMEM((MOST + 1,), jnp.int32),
            pltpu.VMEM((MOST, block_rows, KVH, 2 * HD), jnp.bfloat16),
            pltpu.VMEM((2, max(rows_dev, block_rows) * KVH, HD), jnp.float32),
            pltpu.SemaphoreType.DMA((MOST,)),
        ],
        compiler_params=pltpu.CompilerParams(vmem_limit_bytes=VMEM_LIMIT),
        cost_estimate=pl.CostEstimate(flops=0, bytes_accessed=8 << 20, transcendentals=0),
        name="prepare",
    )(hit, lens, place, pool, span)
    return outs[0], outs[1 : 1 + tp_count], outs[1 + tp_count]


def attend_kernel(
    n_chunks, pool_count, with_span, with_state, final, block_heads, place, lens, counts, query, *refs
):
    refs = list(refs)
    chunk_refs = [[refs.pop(0) for _ in range(pool_count)] for _ in range(n_chunks)]
    span_refs = [refs.pop(0) for _ in range(pool_count)] if with_span else []
    state_in = [refs.pop(0) for _ in range(3)] if with_state else None
    outs = [refs.pop(0) for _ in range(1 if final else 3)]
    keys, valued = refs[:2]
    span_keys, span_valued = refs[2:4] if with_span else (None, None)
    prompt = pl.program_id(1)
    pool_index = place[0]
    rows_dev = query.shape[1]
    block_rows = chunk_refs[0][0].shape[2]
    group = query.shape[2] // HD
    held = keys.dtype

    starts = []
    for relative in range(pool_count):
        start = jnp.int32(0)
        for other in range(counts.shape[0]):
            start += jnp.where(other < prompt, counts[other, relative], 0)
        starts.append(start)
    for chunk in range(n_chunks):
        offset = jnp.int32(0)
        for relative in range(pool_count):
            source = chunk_refs[chunk][relative]

            def bring(index, carry, source=source, offset=offset, start=starts[relative]):
                block = source[start + index, 0].astype(held)
                place_at = pl.ds(pl.multiple_of((offset + index) * block_rows, block_rows), block_rows)
                keys[chunk, place_at, :] = block[:, :HD]
                valued[chunk, place_at, :HD] = block[:, HD:]
                valued[chunk, place_at, HD:] = jnp.ones((block_rows, HD), held)
                return carry

            count = counts[prompt, relative]
            lax.fori_loop(0, count, bring, 0)
            offset += count

        def fill(index, carry):
            place_at = pl.ds(pl.multiple_of(index * block_rows, block_rows), block_rows)
            keys[chunk, place_at, :] = keys[chunk, pl.ds(0, block_rows), :]
            valued[chunk, place_at, :] = jnp.zeros((block_rows, 2 * HD), held)
            return carry

        lax.fori_loop(offset, MAXB, fill, 0)
    if with_span:
        for relative in range(pool_count):
            block = span_refs[relative][0, 0]
            place_at = pl.ds(relative * rows_dev, rows_dev)
            span_keys[place_at, :] = block[:, :HD]
            span_valued[place_at, :HD] = block[:, HD:]
            span_valued[place_at, HD:] = jnp.ones((rows_dev, HD), jnp.bfloat16)

    rows = block_heads * rows_dev
    for first in range(0, group, block_heads):
        heads = range(first, first + block_heads)
        here = pl.ds(first * rows_dev, rows)
        asked = jnp.concatenate([query[0, :, h * HD : (h + 1) * HD] for h in heads], axis=0)
        running = None
        if with_state:
            running = [ref[0, 0, here, :] for ref in state_in]

        def update(running, scores, valued_here):
            peak = jnp.max(scores, axis=1, keepdims=True)
            if running is None:
                new_peak = jnp.broadcast_to(peak, (rows, HD))
            else:
                new_peak = jnp.maximum(running[0], peak)
            weights = jnp.exp2((scores - new_peak[:, :1]) * exponent_scale).astype(jnp.bfloat16)
            result = jnp.dot(weights, valued_here, preferred_element_type=jnp.float32)
            if running is None:
                return [new_peak, result[:, HD:], result[:, :HD]]
            factor = jnp.exp2((running[0] - new_peak) * exponent_scale)
            return [
                new_peak,
                running[1] * factor + result[:, HD:],
                running[2] * factor + result[:, :HD],
            ]

        def score(keys_here):
            return lax.dot_general(
                asked, keys_here, (((1,), (1,)), ((), ())), preferred_element_type=jnp.float32
            )

        if with_span:
            scores = score(span_keys[...])
            columns = lax.broadcasted_iota(jnp.int32, (1, rows_dev), 1)
            key_pos = jnp.concatenate(
                [
                    holder_of(relative, pool_index, pool_count) * rows_dev + columns
                    for relative in range(pool_count)
                ],
                axis=1,
            )
            query_pos = pool_index * rows_dev + lax.rem(
                lax.broadcasted_iota(jnp.int32, (rows, 1), 0), rows_dev
            )
            running = update(
                running, jnp.where(key_pos <= query_pos, scores, lowest), span_valued[...]
            )
        for chunk in range(n_chunks):
            running = update(
                running,
                score(keys[chunk].astype(jnp.bfloat16)),
                valued[chunk].astype(jnp.bfloat16),
            )
        if final:
            attended = (running[2] / running[1]).astype(jnp.bfloat16)
            for at, h in enumerate(heads):
                outs[0][0, :, h * HD : (h + 1) * HD] = attended[at * rows_dev : (at + 1) * rows_dev]
        else:
            for ref, value in zip(outs, running):
                ref[0, 0, here, :] = value


def attend(place, lens, counts, queries, chunks, kv_dev, span=None, state=None, final=False):
    pool_count = len(chunks[0])
    prompts, rows_dev, features = queries.shape
    group = features // HD // kv_dev
    block_rows = chunks[0][0].shape[2]
    key_rows = MAXB * block_rows
    held = jnp.bfloat16 if block_rows % 16 == 0 else jnp.float32
    block_heads = min(2, group)
    query_spec = pl.BlockSpec((1, rows_dev, group * HD), lambda k, p: (p, 0, k))
    chunk_spec = pl.BlockSpec((MOST, 1, block_rows, 2 * HD), lambda k, p: (0, k, 0, 0))
    span_spec = pl.BlockSpec((1, 1, rows_dev, 2 * HD), lambda k, p: (k, p, 0, 0))
    state_spec = pl.BlockSpec((1, 1, group * rows_dev, HD), lambda k, p: (k, p, 0, 0))
    state_shape = jax.ShapeDtypeStruct((kv_dev, prompts, group * rows_dev, HD), jnp.float32)
    operands = [place, lens, counts, queries] + [a for chunk in chunks for a in chunk]
    specs = [SMEM(), SMEM(), SMEM(), query_spec] + [chunk_spec] * (pool_count * len(chunks))
    scratch = [
        pltpu.VMEM((len(chunks), key_rows, HD), held),
        pltpu.VMEM((len(chunks), key_rows, 2 * HD), held),
    ]
    n_keys = key_rows * len(chunks)
    if span is not None:
        operands += span
        specs += [span_spec] * pool_count
        scratch += [
            pltpu.VMEM((pool_count * rows_dev, HD), jnp.bfloat16),
            pltpu.VMEM((pool_count * rows_dev, 2 * HD), jnp.bfloat16),
        ]
        n_keys += pool_count * rows_dev
    if state is not None:
        operands += state
        specs += [state_spec] * 3
    if final:
        out_shape = [jax.ShapeDtypeStruct(queries.shape, jnp.bfloat16)]
        out_specs = [query_spec]
    else:
        out_shape = [state_shape] * 3
        out_specs = [state_spec] * 3
    rows = prompts * rows_dev * kv_dev * group
    return pl.pallas_call(
        functools.partial(
            attend_kernel,
            len(chunks),
            pool_count,
            span is not None,
            state is not None,
            final,
            block_heads,
        ),
        grid=(kv_dev, prompts),
        out_shape=out_shape,
        in_specs=specs,
        out_specs=out_specs,
        scratch_shapes=scratch,
        compiler_params=pltpu.CompilerParams(vmem_limit_bytes=VMEM_LIMIT),
        cost_estimate=pl.CostEstimate(
            flops=rows * n_keys * HD * 6,
            bytes_accessed=8 << 20,
            transcendentals=rows * n_keys,
        ),
        name="attend",
    )(*operands)


def project_kernel(which, attended, weight, out):
    out[...] = jnp.dot(
        attended[...], weight[...], preferred_element_type=jnp.float32
    ).astype(out.dtype)


def project(which, attended, out_w, width, dtype):
    rows, depth = attended.shape
    tile = min(512, width)
    steps = width // tile
    return pl.pallas_call(
        project_kernel,
        grid_spec=pltpu.PrefetchScalarGridSpec(
            num_scalar_prefetch=1,
            grid=(steps,),
            in_specs=[
                pl.BlockSpec((rows, depth), lambda j, which: (0, 0)),
                pl.BlockSpec((depth, tile), lambda j, which: (0, which[0] * steps + j)),
            ],
            out_specs=pl.BlockSpec((rows, tile), lambda j, which: (0, j)),
        ),
        out_shape=jax.ShapeDtypeStruct((rows, width), dtype),
        compiler_params=pltpu.CompilerParams(vmem_limit_bytes=VMEM_LIMIT),
        cost_estimate=pl.CostEstimate(
            flops=2 * rows * depth * width,
            bytes_accessed=2 * depth * width + 4 * rows * width,
            transcendentals=0,
        ),
        name="project",
    )(which.reshape(1), attended, out_w)


def over_pool(array, pool_count):
    gathered = []
    swap = [(i, i ^ 1) for i in range(pool_count)]
    for chips in range(pool_count // 2):
        pairs = [(i, (i + 2 * chips) % pool_count) for i in range(pool_count)]
        arrived = array if chips == 0 else lax.ppermute(array, "pool", pairs)
        gathered += [arrived, lax.ppermute(arrived, "pool", swap)]
    return gathered


def local(
    queries, span_kv, prefix_pool, hit_blocks, prefix_len, dest_blocks, out_w, residual, norm_gain
):
    tp_count = lax.axis_size("tp")
    tp_index = lax.axis_index("tp")
    pool_count = lax.axis_size("pool")
    pool_index = lax.axis_index("pool")
    prompts, rows_dev = queries.shape[:2]
    heads_dev = queries.shape[2] // HD
    kv_dev = max(1, heads_dev // (QH // KVH))
    slots_dev, block_rows = prefix_pool.shape[:2]
    d_dev = residual.shape[2]
    place = jnp.stack([pool_index, tp_index]).astype(jnp.int32)

    counts, sends, span_own = prepare(
        tp_count, pool_count, heads_dev, kv_dev, hit_blocks, prefix_len, place, prefix_pool, span_kv
    )
    chunks = [over_pool(sends[0], pool_count)]
    span = over_pool(span_own, pool_count)
    order = sorted(range(1, tp_count), key=lambda s: min(s, tp_count - s))
    for shift in order:
        pairs = [(i, (i + shift) % tp_count) for i in range(tp_count)]
        chunks.append(over_pool(lax.ppermute(sends[shift], "tp", pairs), pool_count))
    state = attend(place, prefix_len, counts, queries, chunks[:-1], kv_dev, span=span)
    attended = attend(
        place, prefix_len, counts, queries, chunks[-1:], kv_dev, state=state, final=True
    )[0]
    attended = attended.reshape(prompts * rows_dev, heads_dev * HD)

    last = tp_count - 1
    from_left = from_right = None
    for step in range(1, tp_count):
        right_pairs = [(i, i + 1) for i in range(last) if step >= i + 1]
        left_pairs = [(i, i - 1) for i in range(1, tp_count) if step >= tp_count - i]
        to_right = lax.rem(tp_index + tp_count - step, tp_count)
        to_left = lax.rem(tp_index + step, tp_count)
        right_sources = {i for i, _ in right_pairs}
        if right_sources & {i for i, _ in left_pairs}:
            right = project(to_right, attended, out_w, d_dev, jnp.float32)
            left = project(to_left, attended, out_w, d_dev, jnp.float32)
        else:
            cut = max(right_sources)
            which = jnp.where(tp_index <= cut, to_right, to_left)
            first = jnp.bfloat16 if step == 1 else jnp.float32
            right = left = project(which, attended, out_w, d_dev, first)
        parts = []
        for prompt in range(prompts):
            these = slice(prompt * rows_dev, (prompt + 1) * rows_dev)
            going = [right[these], left[these]]
            if step > 1:
                going = [
                    (mine + came[prompt].astype(jnp.float32)).astype(jnp.bfloat16)
                    for mine, came in zip(going, (from_left, from_right))
                ]
            parts.append(
                (lax.ppermute(going[0], "tp", right_pairs), lax.ppermute(going[1], "tp", left_pairs))
            )
        from_left = [part[0] for part in parts]
        from_right = [part[1] for part in parts]
    own = project(tp_index, attended, out_w, d_dev, jnp.float32)
    own = own.reshape(prompts, rows_dev, d_dev) + residual.astype(jnp.float32)

    pieces = span_kv.reshape(
        prompts, rows_dev // block_rows // tp_count, tp_count, block_rows, KVH, 2 * HD
    )
    own_rows = lax.dynamic_index_in_dim(pieces, tp_index, 2, keepdims=False)
    written = lax.all_gather(own_rows, "pool", axis=1, tiled=True)
    written = written.reshape(-1, block_rows, KVH, 2 * HD)
    targets = dest_blocks.reshape(-1)
    slot_ids = pool_index * slots_dev + jnp.arange(slots_dev)
    matching = (targets[None, :] == slot_ids[:, None]).astype(jnp.int32)
    present = jnp.sum(matching, axis=1) > 0
    source = jnp.sum(matching * jnp.arange(targets.shape[0])[None, :], axis=1)
    new_pool = jnp.where(
        present[:, None, None, None], jnp.take(written, source, axis=0), prefix_pool
    )

    hidden = jnp.stack(
        [
            (
                own[prompt]
                + from_left[prompt].astype(jnp.float32)
                + from_right[prompt].astype(jnp.float32)
            ).astype(jnp.bfloat16)
            for prompt in range(prompts)
        ]
    )
    hidden = lax.optimization_barrier(hidden)
    widened = hidden.astype(jnp.float32)
    squares = jnp.sum(widened * widened, axis=2)
    total = squares
    for shift in range(1, tp_count):
        pairs = [(i, (i + shift) % tp_count) for i in range(tp_count)]
        total = total + lax.ppermute(squares, "tp", pairs)
    mean_square = total / (d_dev * tp_count)
    normed = (
        widened
        * lax.rsqrt(mean_square + epsilon)[..., None]
        * norm_gain.astype(jnp.float32)[None, None, :]
    ).astype(jnp.bfloat16)
    return hidden, normed, new_pool


def solution(mesh):
    placed = (
        P("groups", "pool", "tp"),
        P("groups", "pool", None, None),
        P(("groups", "pool"), "tp", None, None),
        P("groups", None),
        P("groups"),
        P("groups", None),
        P("tp", None),
        P("groups", "pool", "tp"),
        P("tp"),
    )
    return jax.shard_map(
        local,
        mesh=mesh,
        in_specs=placed,
        out_specs=(
            P("groups", "pool", "tp"),
            P("groups", "pool", "tp"),
            P(("groups", "pool"), "tp", None, None),
        ),
        check_vma=False,
    )
```

```python
import functools
import math

import jax
import jax.numpy as jnp
from jax import lax
from jax.experimental import pallas as pl
from jax.experimental.pallas import tpu as pltpu
from jax.sharding import PartitionSpec as P

QH = 64
KVH = 8
HD = 128
MAXB = 24
MOST = 12

epsilon = 1e-05
lowest = -1e30
exponent_scale = math.log2(math.e) / math.sqrt(HD)
VMEM_LIMIT = 56 * 1024 * 1024
WEIGHT_PARTS = 4
TILE_CHUNKS = 2

SMEM = functools.partial(pl.BlockSpec, memory_space=pltpu.SMEM)
VMEM = functools.partial(pl.BlockSpec, memory_space=pltpu.VMEM)
ANY = functools.partial(pl.BlockSpec, memory_space=pl.ANY)


def holder_of(relative, pool_index, pool_count):
    chips = pool_count // 2
    chip = lax.rem(pool_index // 2 + chips - relative // 2, chips)
    core = lax.rem(lax.rem(pool_index, 2) + relative % 2, 2)
    return chip * 2 + core


def spread(block, wide):
    rows = block.shape[0]
    for half in range(2):
        wide[half, pl.ds(0, rows * KVH), :] = (
            block[:, :, half * HD : (half + 1) * HD].astype(jnp.float32).reshape(rows * KVH, HD)
        )


def one_head(head, rows, wide):
    here = pl.ds(head, rows, stride=KVH)
    return jnp.concatenate([wide[half, here, :] for half in range(2)], axis=1).astype(jnp.bfloat16)


def first_head(device, heads_dev):
    return device * heads_dev // (QH // KVH)


def prepare_kernel(tp_count, pool_count, heads_dev, hit, lens, place, pool, *refs):
    counts, needed = refs[:2]
    sends = refs[2 : 2 + tp_count]
    own_slots, held, wide, sems = refs[2 + tp_count :]
    prompts = counts.shape[0]
    slots_dev, block_rows = pool.shape[:2]
    kv_dev = sends[0].shape[1]
    pool_index = place[0]
    tp_index = place[1]
    for slot in range(MOST + 1):
        own_slots[slot] = 0
    for prompt in range(prompts):
        for relative in range(pool_count):
            counts[prompt, relative] = 0

        def entry(position, carry, prompt=prompt):
            block = hit[prompt, position]
            holder = block // slots_dev
            chips = pool_count // 2
            chip_away = lax.rem(pool_index // 2 + chips - holder // 2, chips)
            core_away = lax.rem(lax.rem(pool_index, 2) + lax.rem(holder, 2), 2)
            relative = chip_away * 2 + core_away
            counts[prompt, relative] = counts[prompt, relative] + 1

            @pl.when(holder == pool_index)
            def _():
                rank = own_slots[MOST]
                own_slots[rank] = block - holder * slots_dev
                own_slots[MOST] = rank + 1

            return carry

        lax.fori_loop(0, lens[prompt], entry, 0)
    copies = []
    for slot in range(MOST):
        copy = pltpu.make_async_copy(pool.at[own_slots[slot]], held.at[slot], sems.at[slot])
        copy.start()
        copies.append(copy)
    for at in range(tp_count):
        away = jnp.where(tp_index < tp_count // 2, -1 - at, 1 + at)
        needed[at] = lax.rem(tp_index + away + 2 * tp_count, tp_count)
    for slot in range(MOST):
        copies[slot].wait()
        spread(held[slot], wide)
        for shift in range(tp_count):
            head = first_head(lax.rem(tp_index + shift, tp_count), heads_dev)
            for more in range(kv_dev):
                sends[shift][slot, more] = one_head(head + more, block_rows, wide)


def prepare(tp_count, pool_count, heads_dev, kv_dev, hit, lens, place, pool):
    prompts = lens.shape[0]
    block_rows = pool.shape[1]
    send = jax.ShapeDtypeStruct((MOST, kv_dev, block_rows, 2 * HD), jnp.bfloat16)
    counts, needed, *sends = pl.pallas_call(
        functools.partial(prepare_kernel, tp_count, pool_count, heads_dev),
        out_shape=[
            jax.ShapeDtypeStruct((prompts, pool_count), jnp.int32),
            jax.ShapeDtypeStruct((tp_count,), jnp.int32),
        ]
        + [send] * tp_count,
        in_specs=[SMEM(), SMEM(), SMEM(), ANY()],
        out_specs=[SMEM()] * 2 + [VMEM()] * tp_count,
        scratch_shapes=[
            pltpu.SMEM((MOST + 1,), jnp.int32),
            pltpu.VMEM((MOST, block_rows, KVH, 2 * HD), jnp.bfloat16),
            pltpu.VMEM((2, block_rows * KVH, HD), jnp.float32),
            pltpu.SemaphoreType.DMA((MOST,)),
        ],
        compiler_params=pltpu.CompilerParams(vmem_limit_bytes=VMEM_LIMIT),
        cost_estimate=pl.CostEstimate(flops=0, bytes_accessed=8 << 20, transcendentals=0),
        name="prepare",
    )(hit, lens, place, pool)
    return counts, needed, sends


def span_kernel(heads_dev, place, span, heads, pieces, wide):
    prompts, rows_dev = span.shape[:2]
    block_rows = pieces.shape[1]
    tp_index = place[1]
    for prompt in range(prompts):
        here = pl.ds(pl.multiple_of(tp_index * block_rows, block_rows), block_rows)
        pieces[prompt] = span[prompt, here]
        spread(span[prompt], wide)
        for more in range(heads.shape[0]):
            heads[more, prompt] = one_head(first_head(tp_index, heads_dev) + more, rows_dev, wide)


def span_parts(heads_dev, kv_dev, block_rows, place, span):
    prompts, rows_dev = span.shape[:2]
    return pl.pallas_call(
        functools.partial(span_kernel, heads_dev),
        out_shape=[
            jax.ShapeDtypeStruct((kv_dev, prompts, rows_dev, 2 * HD), jnp.bfloat16),
            jax.ShapeDtypeStruct((prompts, block_rows, KVH, 2 * HD), jnp.bfloat16),
        ],
        in_specs=[SMEM(), VMEM()],
        out_specs=[VMEM()] * 2,
        scratch_shapes=[pltpu.VMEM((2, rows_dev * KVH, HD), jnp.float32)],
        compiler_params=pltpu.CompilerParams(vmem_limit_bytes=VMEM_LIMIT),
        cost_estimate=pl.CostEstimate(flops=0, bytes_accessed=2 << 20, transcendentals=0),
        name="span_parts",
    )(place, span)


def attend_kernel(
    which_prompts, n_chunks, pool_count, kv_dev, pieces, with_span, with_state, final, block_heads, *refs
):
    refs = list(refs)
    place, lens, counts, query = [refs.pop(0) for _ in range(4)]
    chunk_refs = [
        [[refs.pop(0) for _ in range(pool_count)] for _ in range(pieces[chunk])]
        for chunk in range(n_chunks)
    ]
    span_refs = [refs.pop(0) for _ in range(pool_count)] if with_span else []
    state_in = refs.pop(0) if with_state else None
    which, out_w = [refs.pop(0) for _ in range(2)] if final else (None, None)
    prompts = len(which_prompts)
    if final:
        attended = [refs.pop(0) for _ in range(prompts)]
        projected = [refs.pop(0) for _ in range(prompts)]
    else:
        state_out = refs.pop(0)
    asked_all, blocks, keys, valued, sems = [refs.pop(0) for _ in range(5)]
    span_blocks, span_keys, span_valued = [refs.pop(0) for _ in range(3)] if with_span else [None] * 3
    state = refs.pop(0) if with_state else None
    weight = refs.pop(0) if final else None
    pool_index = place[0]
    rows_dev = asked_all.shape[1]
    block_rows = blocks.shape[3]
    key_rows = MAXB * block_rows
    group = asked_all.shape[2] // HD // kv_dev
    held = keys.dtype
    rows = block_heads * rows_dev

    started = []

    def start(source, target):
        copy = pltpu.make_async_copy(source, target, sems.at[len(started)])
        copy.start()
        started.append(copy)
        return copy

    brought = []
    for head in range(kv_dev):
        mine = []
        for at, prompt in enumerate(which_prompts):
            if head == 0:
                mine.append(start(query.at[prompt], asked_all.at[at]))
            if with_span:
                mine += [
                    start(span_refs[r].at[head, prompt], span_blocks.at[head, r, at])
                    for r in range(pool_count)
                ]
        for chunk in range(n_chunks):
            split = pieces[chunk] > 1
            for r in range(pool_count):
                source = chunk_refs[chunk][head if split else 0][r]
                mine.append(
                    start(
                        source.at[:, 0 if split else head], blocks.at[head, chunk * pool_count + r]
                    )
                )
        if with_state:
            mine.append(start(state_in.at[head], state.at[head]))
        brought.append(mine)
    late = []
    if final:
        width = weight.shape[1]
        part = weight.shape[0] // WEIGHT_PARTS
        columns = pl.ds(pl.multiple_of(which[0] * width, width), width)
    if with_span:
        place_in = lax.broadcasted_iota(jnp.int32, (1, rows_dev), 1)
        key_pos = jnp.concatenate(
            [holder_of(r, pool_index, pool_count) * rows_dev + place_in for r in range(pool_count)],
            axis=1,
        )
        query_pos = pool_index * rows_dev + lax.rem(
            lax.broadcasted_iota(jnp.int32, (rows, 1), 0), rows_dev
        )

    def gather(head, prompt):
        for chunk in range(n_chunks):
            offset = jnp.int32(0)
            for r in range(pool_count):
                first = jnp.int32(0)
                for other in range(which_prompts[prompt]):
                    first += counts[other, r]

                def bring(index, carry, at=chunk * pool_count + r, first=first, offset=offset):
                    block = blocks[head, at, first + index].astype(held)
                    here = pl.ds(
                        pl.multiple_of((offset + index) * block_rows, block_rows), block_rows
                    )
                    keys[head, prompt, chunk, here, :] = block[:, :HD]
                    valued[head, prompt, chunk, here, :HD] = block[:, HD:]
                    valued[head, prompt, chunk, here, HD:] = jnp.ones((block_rows, HD), held)
                    return carry

                count = counts[which_prompts[prompt], r]
                lax.fori_loop(0, count, bring, 0)
                offset += count

            def fill(index, carry):
                here = pl.ds(pl.multiple_of(index * block_rows, block_rows), block_rows)
                keys[head, prompt, chunk, here, :] = keys[
                    head, prompt, chunk, pl.ds(0, block_rows), :
                ]
                valued[head, prompt, chunk, here, :] = jnp.zeros((block_rows, 2 * HD), held)
                return carry

            lax.fori_loop(offset, MAXB, fill, 0)
        if with_span:
            for r in range(pool_count):
                here = pl.ds(r * rows_dev, rows_dev)
                block = span_blocks[head, r, prompt]
                span_keys[head, prompt, here, :] = block[:, :HD]
                span_valued[head, prompt, here, :HD] = block[:, HD:]
                span_valued[head, prompt, here, HD:] = jnp.ones((rows_dev, HD), jnp.bfloat16)

    def score(head, prompt, first, chunk):
        heads = range(head * group + first, head * group + first + block_heads)
        asked = jnp.concatenate(
            [asked_all[prompt, :, h * HD : (h + 1) * HD] for h in heads], axis=0
        )
        if chunk is None:
            key_part = span_keys[head, prompt]
        else:
            key_part = keys[head, prompt, chunk : chunk + TILE_CHUNKS].reshape(-1, HD)
        key_part = key_part.astype(jnp.bfloat16)
        scores = lax.dot_general(
            asked, key_part, (((1,), (1,)), ((), ())), preferred_element_type=jnp.float32
        )
        if chunk is None:
            return jnp.where(key_pos <= query_pos, scores, lowest)
        return scores

    tiles = ([None] if with_span else []) + list(range(0, n_chunks, TILE_CHUNKS))

    def score_of(head, prompt, first, at):
        return score(head, prompt, first, tiles[at])

    for head in range(kv_dev):
        for copy in brought[head]:
            copy.wait()
        if final and head == 0:
            late = [
                start(out_w.at[pl.ds(i * part, part), columns], weight.at[pl.ds(i * part, part)])
                for i in range(WEIGHT_PARTS)
            ]
        for prompt in range(prompts):
            gather(head, prompt)
        work = [
            (head, prompt, first, at)
            for prompt in range(prompts)
            for first in range(0, group, block_heads)
            for at in range(len(tiles))
        ]
        ahead = score_of(*work[0])
        for n, (_, prompt, first, at) in enumerate(work):
            scores = ahead
            if n + 1 < len(work):
                ahead = score_of(*work[n + 1])
            here = pl.ds(first * rows_dev, rows)
            running = None if at == 0 else running
            if at == 0 and with_state:
                before = state[head, prompt, here, :]
                running = [before[:, 2 * HD - 1 :], before]
            peak = jnp.max(scores, axis=1, keepdims=True)
            if running is not None:
                peak = jnp.maximum(running[0], peak)
            weights = jnp.exp2((scores - peak) * exponent_scale).astype(jnp.bfloat16)
            chunk = tiles[at]
            if chunk is None:
                value_part = span_valued[head, prompt]
            else:
                value_part = valued[head, prompt, chunk : chunk + TILE_CHUNKS].reshape(-1, 2 * HD)
            result = jnp.dot(
                weights, value_part.astype(jnp.bfloat16), preferred_element_type=jnp.float32
            )
            if running is not None:
                result += running[1] * jnp.exp2((running[0] - peak) * exponent_scale)
            running = [peak, result]
            if at < len(tiles) - 1:
                continue
            if not final:
                state_out[head, prompt, here, :HD] = result[:, :HD]
                lanes = lax.broadcasted_iota(jnp.int32, (rows, HD), 1)
                state_out[head, prompt, here, HD:] = jnp.where(lanes < HD // 2, result[:, HD:], peak)
                continue
            total = result[:, HD : HD + 1] if with_state else result[:, HD:]
            done = (result[:, :HD] / total).astype(jnp.bfloat16)
            for m in range(block_heads):
                h = head * group + first + m
                attended[prompt][:, h * HD : (h + 1) * HD] = done[m * rows_dev : (m + 1) * rows_dev]
    for copy in late:
        copy.wait()
    if final:
        together = jnp.concatenate([ref[...] for ref in attended], axis=0)
        tile = min(512, width)
        for at in range(0, width, tile):
            total = jnp.dot(
                together, weight[:, at : at + tile], preferred_element_type=jnp.float32
            ).astype(jnp.bfloat16)
            for prompt in range(prompts):
                projected[prompt][:, at : at + tile] = total[
                    prompt * rows_dev : (prompt + 1) * rows_dev
                ]


def attend(
    which_prompts, place, lens, counts, queries, chunks, kv_dev, span=None, state=None, out_w=None, which=None, width=0
):
    pool_count = len(chunks[0][0])
    n_chunks = len(chunks)
    prompts = len(which_prompts)
    rows_dev, features = queries.shape[1:]
    group = features // HD // kv_dev
    block_rows = chunks[0][0][0].shape[2]
    key_rows = MAXB * block_rows
    held = jnp.bfloat16 if block_rows % 16 == 0 else jnp.float32
    block_heads = min(8, group)
    final = out_w is not None
    state_shape = (kv_dev, prompts, group * rows_dev, 2 * HD)
    operands = [place, lens, counts, queries]
    operands += [array for chunk in chunks for piece in chunk for array in piece]
    copies = prompts + kv_dev * n_chunks * pool_count
    n_keys = key_rows * n_chunks
    scratch = [
        pltpu.VMEM((prompts, rows_dev, features), jnp.bfloat16),
        pltpu.VMEM((kv_dev, n_chunks * pool_count, MOST, block_rows, 2 * HD), jnp.bfloat16),
        pltpu.VMEM((kv_dev, prompts, n_chunks, key_rows, HD), held),
        pltpu.VMEM((kv_dev, prompts, n_chunks, key_rows, 2 * HD), held),
    ]
    later = []
    if span is not None:
        operands += span
        copies += prompts * kv_dev * pool_count
        n_keys += pool_count * rows_dev
        later += [
            pltpu.VMEM((kv_dev, pool_count, prompts, rows_dev, 2 * HD), jnp.bfloat16),
            pltpu.VMEM((kv_dev, prompts, pool_count * rows_dev, HD), jnp.bfloat16),
            pltpu.VMEM((kv_dev, prompts, pool_count * rows_dev, 2 * HD), jnp.bfloat16),
        ]
    if state is not None:
        operands.append(state)
        copies += kv_dev
        later.append(pltpu.VMEM(state_shape, jnp.float32))
    specs = [SMEM()] * 3 + [ANY()] * (len(operands) - 3)
    if final:
        operands += [which, out_w]
        specs += [SMEM(), ANY()]
        copies += WEIGHT_PARTS
        later.append(pltpu.VMEM((features, width), jnp.bfloat16))
        out_shape = [jax.ShapeDtypeStruct((rows_dev, features), jnp.bfloat16)] * prompts
        out_shape += [jax.ShapeDtypeStruct((rows_dev, width), jnp.bfloat16)] * prompts
    else:
        out_shape = [jax.ShapeDtypeStruct(state_shape, jnp.float32)]
    rows = prompts * rows_dev * kv_dev * group
    return pl.pallas_call(
        functools.partial(
            attend_kernel,
            which_prompts,
            n_chunks,
            pool_count,
            kv_dev,
            [len(chunk) for chunk in chunks],
            span is not None,
            state is not None,
            final,
            block_heads,
        ),
        out_shape=out_shape,
        in_specs=specs,
        out_specs=[VMEM()] * len(out_shape),
        scratch_shapes=scratch + [pltpu.SemaphoreType.DMA((copies,))] + later,
        compiler_params=pltpu.CompilerParams(vmem_limit_bytes=VMEM_LIMIT),
        cost_estimate=pl.CostEstimate(
            flops=rows * n_keys * HD * 6 + 2 * prompts * rows_dev * features * width,
            bytes_accessed=16 << 20,
            transcendentals=rows * n_keys,
        ),
        name="attend",
    )(*operands)


def project_kernel(which, *refs):
    *attended, weight, out = refs
    together = jnp.concatenate([ref[...] for ref in attended], axis=0)
    out[0] = jnp.dot(together, weight[...], preferred_element_type=jnp.float32).astype(out.dtype)


def project(which, skipped, attended, out_w, width):
    rows_dev, depth = attended[0].shape
    rows = rows_dev * len(attended)
    tile = min(1024, width)
    steps = width // tile
    count = which.shape[0] - skipped
    return pl.pallas_call(
        project_kernel,
        grid_spec=pltpu.PrefetchScalarGridSpec(
            num_scalar_prefetch=1,
            grid=(count, steps),
            in_specs=[
                pl.BlockSpec((rows_dev, depth), lambda i, j, which: (0, 0)) for _ in attended
            ]
            + [
                pl.BlockSpec((depth, tile), lambda i, j, which: (0, which[i + skipped] * steps + j)),
            ],
            out_specs=pl.BlockSpec((1, rows, tile), lambda i, j, which: (i, 0, j)),
        ),
        out_shape=jax.ShapeDtypeStruct((count, rows, width), jnp.bfloat16),
        compiler_params=pltpu.CompilerParams(vmem_limit_bytes=VMEM_LIMIT),
        cost_estimate=pl.CostEstimate(
            flops=2 * rows * depth * width * count,
            bytes_accessed=(2 * depth + 4 * rows) * width * count,
            transcendentals=0,
        ),
        name="project",
    )(which, *attended, out_w)


def add_kernel(with_begun, which, partial, *refs):
    total = partial[0].astype(jnp.float32)
    if with_begun:
        total = jnp.where(which[0] < 0, refs[0][...].astype(jnp.float32), total)
    for ref in refs[with_begun:-1]:
        total += ref[...].astype(jnp.float32)
    refs[-1][...] = total.astype(refs[-1].dtype)


def add(which, partials, prompt, came, begun=None):
    rows, width = came[0].shape
    spec = pl.BlockSpec((rows, width), lambda i, which: (0, 0))
    others = ([] if begun is None else [begun]) + came
    return pl.pallas_call(
        functools.partial(add_kernel, int(begun is not None)),
        grid_spec=pltpu.PrefetchScalarGridSpec(
            num_scalar_prefetch=1,
            grid=(1,),
            in_specs=[
                pl.BlockSpec(
                    (1, rows, width), lambda i, which: (jnp.maximum(which[0], 0), prompt, 0)
                )
            ]
            + [spec] * len(others),
            out_specs=spec,
        ),
        out_shape=jax.ShapeDtypeStruct((rows, width), jnp.bfloat16),
        compiler_params=pltpu.CompilerParams(vmem_limit_bytes=VMEM_LIMIT),
        cost_estimate=pl.CostEstimate(
            flops=rows * width, bytes_accessed=8 * rows * width, transcendentals=0
        ),
        name="add",
    )(which.reshape(1), partials, *others)


def over_pool(array, pool_count, after=None):
    gathered = []
    swap = [(i, i ^ 1) for i in range(pool_count)]
    for chips in range(pool_count // 2):
        pairs = [(i, (i + 2 * chips) % pool_count) for i in range(pool_count)]
        arrived = array if chips == 0 else lax.ppermute(array, "pool", pairs)
        passed = arrived
        if after is not None and chips > 0:
            passed, _ = lax.optimization_barrier((arrived, after))
        gathered += [arrived, lax.ppermute(passed, "pool", swap)]
    return gathered


def local(
    queries, span_kv, prefix_pool, hit_blocks, prefix_len, dest_blocks, out_w, residual, norm_gain
):
    tp_count = lax.axis_size("tp")
    tp_index = lax.axis_index("tp")
    pool_count = lax.axis_size("pool")
    pool_index = lax.axis_index("pool")
    prompts, rows_dev = queries.shape[:2]
    heads_dev = queries.shape[2] // HD
    kv_dev = max(1, heads_dev // (QH // KVH))
    slots_dev, block_rows = prefix_pool.shape[:2]
    d_dev = residual.shape[2]
    place = jnp.stack([pool_index, tp_index]).astype(jnp.int32)

    counts, needed, sends = prepare(
        tp_count, pool_count, heads_dev, kv_dev, hit_blocks, prefix_len, place, prefix_pool
    )
    span_own, own_rows = span_parts(heads_dev, kv_dev, block_rows, place, span_kv)
    order = sorted(range(1, tp_count), key=lambda s: -min(s, tp_count - s))
    chunks = [[over_pool(sends[0], pool_count)]]
    span = over_pool(span_own, pool_count)
    along, across = None, [chunks[0][0][2]]
    for at, shift in enumerate(order):
        pairs = [(i, (i + shift) % tp_count) for i in range(tp_count)]
        block = sends[shift]
        if at > 0:
            block, _ = lax.optimization_barrier((block, (along, across[at - 1])))
        along = lax.ppermute(block, "tp", pairs)
        passed, _ = lax.optimization_barrier((along, across[at] if at > 0 else span[2]))
        chunks.append([over_pool(passed, pool_count)])
        across.append(chunks[-1][0][2])

    last = tp_count - 1
    down = tp_index < tp_count // 2
    outs = attend(
        tuple(range(prompts)),
        place,
        prefix_len,
        counts,
        queries,
        chunks,
        kv_dev,
        span=span,
        out_w=out_w,
        which=needed,
        width=d_dev,
    )
    attended, came = outs[:prompts], outs[prompts:]

    def right_pairs(step):
        return [(i, i + 1) for i in range(last) if step >= i + 1]

    def left_pairs(step):
        return [(i, i - 1) for i in range(1, tp_count) if step >= tp_count - i]

    def is_single(step):
        return not {i for i, _ in right_pairs(step)} & {i for i, _ in left_pairs(step)}

    def send(to_right, to_left, step):
        right, left = right_pairs(step), left_pairs(step)
        if to_right is to_left and not {t for _, t in right} & {t for _, t in left}:
            return [lax.ppermute(to_right, "tp", right + left)]
        return [lax.ppermute(to_right, "tp", right), lax.ppermute(to_left, "tp", left)]

    written = lax.all_gather(own_rows[:, None], "pool", axis=1, tiled=True)
    written = written.reshape(-1, block_rows, KVH, 2 * HD)
    targets = dest_blocks.reshape(-1)
    slot_ids = pool_index * slots_dev + jnp.arange(slots_dev)
    matching = (targets[None, :] == slot_ids[:, None]).astype(jnp.int32)
    present = jnp.sum(matching, axis=1) > 0
    source = jnp.sum(matching * jnp.arange(targets.shape[0])[None, :], axis=1)
    new_pool = jnp.where(
        present[:, None, None, None], jnp.take(written, source, axis=0), prefix_pool
    )

    partials = project(needed, 1, attended, out_w, d_dev)
    begun, came = came, [send(block, block, 1) for block in came]
    for step in range(2, tp_count):
        main, other = step - 2, tp_count - step - 2
        for prompt in range(prompts):
            if step == tp_count - 1 and prompt == 0:
                came[0], new_pool = lax.optimization_barrier((came[0], new_pool))
            if is_single(step):
                block = add(jnp.int32(main), partials, prompt, came[prompt])
                came[prompt] = send(block, block, step)
                continue
            to_right, to_left = [
                add(
                    jnp.where(ours, main, other).astype(jnp.int32),
                    partials,
                    prompt,
                    [arrived],
                    begun[prompt] if other < 0 else None,
                )
                for ours, arrived in zip((down, ~down), came[prompt])
            ]
            came[prompt] = send(to_right, to_left, step)

    hidden = jnp.stack(
        [
            (
                partials[tp_count - 2, prompt * rows_dev : (prompt + 1) * rows_dev].astype(jnp.float32)
                + came[prompt][0].astype(jnp.float32)
                + came[prompt][1].astype(jnp.float32)
                + residual[prompt].astype(jnp.float32)
            ).astype(jnp.bfloat16)
            for prompt in range(prompts)
        ]
    )
    hidden = lax.optimization_barrier(hidden)
    widened = hidden.astype(jnp.float32)
    squares = jnp.sum(widened * widened, axis=2)
    total = squares
    for shift in range(1, tp_count):
        pairs = [(i, (i + shift) % tp_count) for i in range(tp_count)]
        total = total + lax.ppermute(squares, "tp", pairs)
    mean_square = total / (d_dev * tp_count)
    normed = (
        widened
        * lax.rsqrt(mean_square + epsilon)[..., None]
        * norm_gain.astype(jnp.float32)[None, None, :]
    ).astype(jnp.bfloat16)
    return hidden, normed, new_pool


def solution(mesh):
    placed = (
        P("groups", "pool", "tp"),
        P("groups", "pool", None, None),
        P(("groups", "pool"), "tp", None, None),
        P("groups", None),
        P("groups"),
        P("groups", None),
        P("tp", None),
        P("groups", "pool", "tp"),
        P("tp"),
    )
    return jax.shard_map(
        local,
        mesh=mesh,
        in_specs=placed,
        out_specs=(
            P("groups", "pool", "tp"),
            P("groups", "pool", "tp"),
            P(("groups", "pool"), "tp", None, None),
        ),
        check_vma=False,
    )
```

```python
import functools
import math

import jax
import jax.numpy as jnp
from jax import lax
from jax.experimental import pallas as pl
from jax.experimental.pallas import tpu as pltpu
from jax.sharding import PartitionSpec as P

QH = 64
KVH = 8
HD = 128
MAXB = 24
MOST = 12

epsilon = 1e-05
lowest = -1e30
exponent_scale = math.log2(math.e) / math.sqrt(HD)
VMEM_LIMIT = 56 * 1024 * 1024
WEIGHT_PARTS = 4
TILE_CHUNKS = 2

SMEM = functools.partial(pl.BlockSpec, memory_space=pltpu.SMEM)
VMEM = functools.partial(pl.BlockSpec, memory_space=pltpu.VMEM)
ANY = functools.partial(pl.BlockSpec, memory_space=pl.ANY)


def holder_of(relative, pool_index, pool_count):
    chips = pool_count // 2
    chip = lax.rem(pool_index // 2 + chips - relative // 2, chips)
    core = lax.rem(lax.rem(pool_index, 2) + relative % 2, 2)
    return chip * 2 + core


def spread(block, wide):
    rows = block.shape[0]
    for half in range(2):
        wide[half, pl.ds(0, rows * KVH), :] = (
            block[:, :, half * HD : (half + 1) * HD].astype(jnp.float32).reshape(rows * KVH, HD)
        )


def one_head(head, rows, wide):
    here = pl.ds(head, rows, stride=KVH)
    return jnp.concatenate([wide[half, here, :] for half in range(2)], axis=1).astype(jnp.bfloat16)


def first_head(device, heads_dev):
    return device * heads_dev // (QH // KVH)


def prepare_kernel(tp_count, pool_count, heads_dev, hit, lens, pool, *refs):
    counts, needed, *sends, own_slots, held, wide, sems = refs
    prompts = counts.shape[0]
    slots_dev, block_rows = pool.shape[:2]
    kv_dev = sends[0].shape[1]
    pool_index = lax.axis_index("pool")
    tp_index = lax.axis_index("tp")
    for slot in range(MOST + 1):
        own_slots[slot] = 0
    for prompt in range(prompts):
        for relative in range(pool_count):
            counts[prompt, relative] = 0

        def entry(position, carry, prompt=prompt):
            block = hit[prompt, position]
            holder = block // slots_dev
            chips = pool_count // 2
            chip_away = lax.rem(pool_index // 2 + chips - holder // 2, chips)
            core_away = lax.rem(lax.rem(pool_index, 2) + lax.rem(holder, 2), 2)
            relative = chip_away * 2 + core_away
            counts[prompt, relative] = counts[prompt, relative] + 1

            @pl.when(holder == pool_index)
            def _():
                rank = own_slots[MOST]
                own_slots[rank] = block - holder * slots_dev
                own_slots[MOST] = rank + 1

            return carry

        lax.fori_loop(0, lens[prompt], entry, 0)
    copies = []
    for slot in range(MOST):
        copy = pltpu.make_async_copy(pool.at[own_slots[slot]], held.at[slot], sems.at[slot])
        copy.start()
        copies.append(copy)
    for at in range(tp_count):
        away = jnp.where(tp_index < tp_count // 2, -1 - at, 1 + at)
        needed[at] = lax.rem(tp_index + away + 2 * tp_count, tp_count)
    for slot in range(MOST):
        copies[slot].wait()
        spread(held[slot], wide)
        for shift in range(tp_count):
            head = first_head(lax.rem(tp_index + shift, tp_count), heads_dev)
            for more in range(kv_dev):
                sends[shift][slot, more] = one_head(head + more, block_rows, wide)


def prepare(tp_count, pool_count, heads_dev, kv_dev, hit, lens, pool):
    prompts = lens.shape[0]
    block_rows = pool.shape[1]
    send = jax.ShapeDtypeStruct((MOST, kv_dev, block_rows, 2 * HD), jnp.bfloat16)
    counts, needed, *sends = pl.pallas_call(
        functools.partial(prepare_kernel, tp_count, pool_count, heads_dev),
        out_shape=[
            jax.ShapeDtypeStruct((prompts, pool_count), jnp.int32),
            jax.ShapeDtypeStruct((tp_count,), jnp.int32),
        ]
        + [send] * tp_count,
        in_specs=[SMEM(), SMEM(), ANY()],
        out_specs=[SMEM()] * 2 + [VMEM()] * tp_count,
        scratch_shapes=[
            pltpu.SMEM((MOST + 1,), jnp.int32),
            pltpu.VMEM((MOST, block_rows, KVH, 2 * HD), jnp.bfloat16),
            pltpu.VMEM((2, (block_rows + 1) * KVH, HD), jnp.float32),
            pltpu.SemaphoreType.DMA((MOST,)),
        ],
        compiler_params=pltpu.CompilerParams(vmem_limit_bytes=VMEM_LIMIT),
        cost_estimate=pl.CostEstimate(flops=0, bytes_accessed=8 << 20, transcendentals=0),
        name="prepare",
    )(hit, lens, pool)
    return counts, needed, sends


def span_kernel(heads_dev, span, heads, pieces, wide):
    prompts, rows_dev = span.shape[:2]
    block_rows = pieces.shape[1]
    tp_index = lax.axis_index("tp")
    for prompt in range(prompts):
        here = pl.ds(pl.multiple_of(tp_index * block_rows, block_rows), block_rows)
        pieces[prompt] = span[prompt, here]
        spread(span[prompt], wide)
        for more in range(heads.shape[0]):
            heads[more, prompt] = one_head(first_head(tp_index, heads_dev) + more, rows_dev, wide)


def span_parts(heads_dev, kv_dev, block_rows, span):
    prompts, rows_dev = span.shape[:2]
    return pl.pallas_call(
        functools.partial(span_kernel, heads_dev),
        out_shape=[
            jax.ShapeDtypeStruct((kv_dev, prompts, rows_dev, 2 * HD), jnp.bfloat16),
            jax.ShapeDtypeStruct((prompts, block_rows, KVH, 2 * HD), jnp.bfloat16),
        ],
        in_specs=[VMEM()],
        out_specs=[VMEM()] * 2,
        scratch_shapes=[pltpu.VMEM((2, (rows_dev + 1) * KVH, HD), jnp.float32)],
        compiler_params=pltpu.CompilerParams(vmem_limit_bytes=VMEM_LIMIT),
        cost_estimate=pl.CostEstimate(flops=0, bytes_accessed=2 << 20, transcendentals=0),
        name="span_parts",
    )(span)


def attend_kernel(
    which_prompts, n_chunks, pool_count, kv_dev, pieces, with_span, with_state, final, block_heads, *refs
):
    refs = list(refs)
    counts, query = [refs.pop(0) for _ in range(2)]
    chunk_refs = [
        [[refs.pop(0) for _ in range(pool_count)] for _ in range(pieces[chunk])]
        for chunk in range(n_chunks)
    ]
    span_refs = [refs.pop(0) for _ in range(pool_count)] if with_span else []
    state_in = refs.pop(0) if with_state else None
    which, out_w = [refs.pop(0) for _ in range(2)] if final else (None, None)
    prompts = len(which_prompts)
    if final:
        attended = [refs.pop(0) for _ in range(prompts)]
        projected = [refs.pop(0) for _ in range(prompts)]
    else:
        state_out = refs.pop(0)
    asked_all, blocks, keys, valued, sems = [refs.pop(0) for _ in range(5)]
    span_blocks, span_keys, span_valued = [refs.pop(0) for _ in range(3)] if with_span else [None] * 3
    state = refs.pop(0) if with_state else None
    weight = refs.pop(0) if final else None
    pool_index = lax.axis_index("pool")
    rows_dev = asked_all.shape[1]
    block_rows = blocks.shape[3]
    key_rows = MAXB * block_rows
    group = asked_all.shape[2] // HD // kv_dev
    held = keys.dtype
    rows = block_heads * rows_dev

    started = []

    def start(source, target):
        copy = pltpu.make_async_copy(source, target, sems.at[len(started)])
        copy.start()
        started.append(copy)
        return copy

    asking = [start(query.at[prompt], asked_all.at[at]) for at, prompt in enumerate(which_prompts)]
    brought_span, brought = [], []
    for head in range(kv_dev):
        mine = []
        if with_span:
            for at, prompt in enumerate(which_prompts):
                mine += [
                    start(span_refs[r].at[head, prompt], span_blocks.at[head, r, at])
                    for r in range(pool_count)
                ]
        if with_state:
            mine.append(start(state_in.at[head], state.at[head]))
        brought_span.append(mine)
        brought.append([])
        for chunk in range(n_chunks):
            split = pieces[chunk] > 1
            brought[head].append(
                [
                    start(
                        chunk_refs[chunk][head if split else 0][r].at[:, 0 if split else head],
                        blocks.at[head, chunk * pool_count + r],
                    )
                    for r in range(pool_count)
                ]
            )
    late = []
    if final:
        width = weight.shape[1]
        part = weight.shape[0] // WEIGHT_PARTS
        columns = pl.ds(pl.multiple_of(which[0] * width, width), width)
    if with_span:
        place_in = lax.broadcasted_iota(jnp.int32, (1, rows_dev), 1)
        key_pos = jnp.concatenate(
            [holder_of(r, pool_index, pool_count) * rows_dev + place_in for r in range(pool_count)],
            axis=1,
        )
        query_pos = pool_index * rows_dev + lax.rem(
            lax.broadcasted_iota(jnp.int32, (rows, 1), 0), rows_dev
        )

    def gather(head, prompt, chunk):
        if chunk is not None:
            offset = jnp.int32(0)
            for r in range(pool_count):
                first = jnp.int32(0)
                for other in range(which_prompts[prompt]):
                    first += counts[other, r]

                def bring(index, carry, at=chunk * pool_count + r, first=first, offset=offset):
                    block = blocks[head, at, first + index].astype(held)
                    here = pl.ds(
                        pl.multiple_of((offset + index) * block_rows, block_rows), block_rows
                    )
                    keys[head, prompt, chunk, here, :] = block[:, :HD]
                    valued[head, prompt, chunk, here, :HD] = block[:, HD:]
                    valued[head, prompt, chunk, here, HD:] = jnp.ones((block_rows, HD), held)
                    return carry

                count = counts[which_prompts[prompt], r]
                lax.fori_loop(0, count, bring, 0)
                offset += count

            def fill(index, carry):
                here = pl.ds(pl.multiple_of(index * block_rows, block_rows), block_rows)
                keys[head, prompt, chunk, here, :] = keys[
                    head, prompt, chunk, pl.ds(0, block_rows), :
                ]
                valued[head, prompt, chunk, here, :] = jnp.zeros((block_rows, 2 * HD), held)
                return carry

            lax.fori_loop(offset, MAXB, fill, 0)
        else:
            for r in range(pool_count):
                here = pl.ds(r * rows_dev, rows_dev)
                block = span_blocks[head, r, prompt]
                span_keys[head, prompt, here, :] = block[:, :HD]
                span_valued[head, prompt, here, :HD] = block[:, HD:]
                span_valued[head, prompt, here, HD:] = jnp.ones((rows_dev, HD), jnp.bfloat16)

    def score(head, prompt, first, chunk):
        heads = range(head * group + first, head * group + first + block_heads)
        asked = jnp.concatenate(
            [asked_all[prompt, :, h * HD : (h + 1) * HD] for h in heads], axis=0
        )
        if chunk is None:
            key_part = span_keys[head, prompt]
        else:
            key_part = keys[head, prompt, chunk : chunk + TILE_CHUNKS].reshape(-1, HD)
        key_part = key_part.astype(jnp.bfloat16)
        scores = lax.dot_general(
            asked, key_part, (((1,), (1,)), ((), ())), preferred_element_type=jnp.float32
        )
        if chunk is None:
            return jnp.where(key_pos <= query_pos, scores, lowest)
        return scores

    tiles = ([None] if with_span else []) + list(range(0, n_chunks, TILE_CHUNKS))

    def score_of(head, prompt, first, at):
        return score(head, prompt, first, tiles[at])

    for head in range(kv_dev):
        for copy in brought_span[head] + (asking if head == 0 else []):
            copy.wait()
        if with_span:
            for prompt in range(prompts):
                gather(head, prompt, None)
        for chunk in range(n_chunks):
            for copy in brought[head][chunk]:
                copy.wait()
            for prompt in range(prompts):
                gather(head, prompt, chunk)
        if final and head == 0:
            late = [
                start(out_w.at[pl.ds(i * part, part), columns], weight.at[pl.ds(i * part, part)])
                for i in range(WEIGHT_PARTS)
            ]
        work = [
            (head, prompt, first, at)
            for prompt in range(prompts)
            for first in range(0, group, block_heads)
            for at in range(len(tiles))
        ]
        ahead = score_of(*work[0])
        for n, (_, prompt, first, at) in enumerate(work):
            scores = ahead
            if n + 1 < len(work):
                ahead = score_of(*work[n + 1])
            here = pl.ds(first * rows_dev, rows)
            running = None if at == 0 else running
            if at == 0 and with_state:
                before = state[head, prompt, here, :]
                running = [before[:, 2 * HD - 1 :], before]
            peak = jnp.max(scores, axis=1, keepdims=True)
            if running is not None:
                peak = jnp.maximum(running[0], peak)
            weights = jnp.exp2((scores - peak) * exponent_scale).astype(jnp.bfloat16)
            chunk = tiles[at]
            if chunk is None:
                value_part = span_valued[head, prompt]
            else:
                value_part = valued[head, prompt, chunk : chunk + TILE_CHUNKS].reshape(-1, 2 * HD)
            result = jnp.dot(
                weights, value_part.astype(jnp.bfloat16), preferred_element_type=jnp.float32
            )
            if running is not None:
                result += running[1] * jnp.exp2((running[0] - peak) * exponent_scale)
            running = [peak, result]
            if at < len(tiles) - 1:
                continue
            if not final:
                state_out[head, prompt, here, :HD] = result[:, :HD]
                lanes = lax.broadcasted_iota(jnp.int32, (rows, HD), 1)
                state_out[head, prompt, here, HD:] = jnp.where(lanes < HD // 2, result[:, HD:], peak)
                continue
            total = result[:, HD : HD + 1] if with_state else result[:, HD:]
            done = (result[:, :HD] / total).astype(jnp.bfloat16)
            for m in range(block_heads):
                h = head * group + first + m
                attended[prompt][:, h * HD : (h + 1) * HD] = done[m * rows_dev : (m + 1) * rows_dev]
    for copy in late:
        copy.wait()
    if final:
        together = jnp.concatenate([ref[...] for ref in attended], axis=0)
        tile = min(512, width)
        for at in range(0, width, tile):
            total = jnp.dot(
                together, weight[:, at : at + tile], preferred_element_type=jnp.float32
            ).astype(jnp.bfloat16)
            for prompt in range(prompts):
                projected[prompt][:, at : at + tile] = total[
                    prompt * rows_dev : (prompt + 1) * rows_dev
                ]


def attend(
    which_prompts, counts, queries, chunks, kv_dev, span=None, state=None, out_w=None, which=None, width=0
):
    pool_count = len(chunks[0][0])
    n_chunks = len(chunks)
    prompts = len(which_prompts)
    rows_dev, features = queries.shape[1:]
    group = features // HD // kv_dev
    block_rows = chunks[0][0][0].shape[2]
    key_rows = MAXB * block_rows
    held = jnp.bfloat16 if block_rows % 16 == 0 else jnp.float32
    block_heads = min(8, group)
    final = out_w is not None
    state_shape = (kv_dev, prompts, group * rows_dev, 2 * HD)
    operands = [counts, queries]
    operands += [array for chunk in chunks for piece in chunk for array in piece]
    copies = prompts + kv_dev * n_chunks * pool_count
    n_keys = key_rows * n_chunks
    scratch = [
        pltpu.VMEM((prompts, rows_dev, features), jnp.bfloat16),
        pltpu.VMEM((kv_dev, n_chunks * pool_count, MOST, block_rows, 2 * HD), jnp.bfloat16),
        pltpu.VMEM((kv_dev, prompts, n_chunks, key_rows, HD), held),
        pltpu.VMEM((kv_dev, prompts, n_chunks, key_rows, 2 * HD), held),
    ]
    later = []
    if span is not None:
        operands += span
        copies += prompts * kv_dev * pool_count
        n_keys += pool_count * rows_dev
        later += [
            pltpu.VMEM((kv_dev, pool_count, prompts, rows_dev, 2 * HD), jnp.bfloat16),
            pltpu.VMEM((kv_dev, prompts, pool_count * rows_dev, HD), jnp.bfloat16),
            pltpu.VMEM((kv_dev, prompts, pool_count * rows_dev, 2 * HD), jnp.bfloat16),
        ]
    if state is not None:
        operands.append(state)
        copies += kv_dev
        later.append(pltpu.VMEM(state_shape, jnp.float32))
    specs = [SMEM()] + [ANY()] * (len(operands) - 1)
    if final:
        operands += [which, out_w]
        specs += [SMEM(), ANY()]
        copies += WEIGHT_PARTS
        later.append(pltpu.VMEM((features, width), jnp.bfloat16))
        out_shape = [jax.ShapeDtypeStruct((rows_dev, features), jnp.bfloat16)] * prompts
        out_shape += [jax.ShapeDtypeStruct((rows_dev, width), jnp.bfloat16)] * prompts
    else:
        out_shape = [jax.ShapeDtypeStruct(state_shape, jnp.float32)]
    rows = prompts * rows_dev * kv_dev * group
    return pl.pallas_call(
        functools.partial(
            attend_kernel,
            which_prompts,
            n_chunks,
            pool_count,
            kv_dev,
            [len(chunk) for chunk in chunks],
            span is not None,
            state is not None,
            final,
            block_heads,
        ),
        out_shape=out_shape,
        in_specs=specs,
        out_specs=[VMEM()] * len(out_shape),
        scratch_shapes=scratch + [pltpu.SemaphoreType.DMA((copies,))] + later,
        compiler_params=pltpu.CompilerParams(vmem_limit_bytes=VMEM_LIMIT),
        cost_estimate=pl.CostEstimate(
            flops=rows * n_keys * HD * 6 + 2 * prompts * rows_dev * features * width,
            bytes_accessed=16 << 20,
            transcendentals=rows * n_keys,
        ),
        name="attend",
    )(*operands)


def project_kernel(which, *refs):
    *attended, weight, out = refs
    together = jnp.concatenate([ref[...] for ref in attended], axis=0)
    out[0] = jnp.dot(together, weight[...], preferred_element_type=jnp.float32).astype(out.dtype)


def project(which, skipped, attended, out_w, width):
    rows_dev, depth = attended[0].shape
    rows = rows_dev * len(attended)
    tile = min(1024, width)
    steps = width // tile
    count = which.shape[0] - skipped
    return pl.pallas_call(
        project_kernel,
        grid_spec=pltpu.PrefetchScalarGridSpec(
            num_scalar_prefetch=1,
            grid=(count, steps),
            in_specs=[
                pl.BlockSpec((rows_dev, depth), lambda i, j, which: (0, 0)) for _ in attended
            ]
            + [
                pl.BlockSpec((depth, tile), lambda i, j, which: (0, which[i + skipped] * steps + j)),
            ],
            out_specs=pl.BlockSpec((1, rows, tile), lambda i, j, which: (i, 0, j)),
        ),
        out_shape=jax.ShapeDtypeStruct((count, rows, width), jnp.bfloat16),
        compiler_params=pltpu.CompilerParams(vmem_limit_bytes=VMEM_LIMIT),
        cost_estimate=pl.CostEstimate(
            flops=2 * rows * depth * width * count,
            bytes_accessed=(2 * depth + 4 * rows) * width * count,
            transcendentals=0,
        ),
        name="project",
    )(which, *attended, out_w)


def add_kernel(with_begun, which, partial, *refs):
    total = partial[0].astype(jnp.float32)
    if with_begun:
        total = jnp.where(which[0] < 0, refs[0][...].astype(jnp.float32), total)
    for ref in refs[with_begun:-1]:
        total += ref[...].astype(jnp.float32)
    refs[-1][...] = total.astype(refs[-1].dtype)


def add(which, partials, prompt, came, begun=None):
    rows, width = came[0].shape
    spec = pl.BlockSpec((rows, width), lambda i, which: (0, 0))
    others = ([] if begun is None else [begun]) + came
    return pl.pallas_call(
        functools.partial(add_kernel, int(begun is not None)),
        grid_spec=pltpu.PrefetchScalarGridSpec(
            num_scalar_prefetch=1,
            grid=(1,),
            in_specs=[
                pl.BlockSpec(
                    (1, rows, width), lambda i, which: (jnp.maximum(which[0], 0), prompt, 0)
                )
            ]
            + [spec] * len(others),
            out_specs=spec,
        ),
        out_shape=jax.ShapeDtypeStruct((rows, width), jnp.bfloat16),
        compiler_params=pltpu.CompilerParams(vmem_limit_bytes=VMEM_LIMIT),
        cost_estimate=pl.CostEstimate(
            flops=rows * width, bytes_accessed=8 * rows * width, transcendentals=0
        ),
        name="add",
    )(which.reshape(1), partials, *others)


def over_pool(array, pool_count, after=None):
    gathered = []
    swap = [(i, i ^ 1) for i in range(pool_count)]
    for chips in range(pool_count // 2):
        pairs = [(i, (i + 2 * chips) % pool_count) for i in range(pool_count)]
        arrived = array if chips == 0 else lax.ppermute(array, "pool", pairs)
        passed = arrived
        if after is not None and chips > 0:
            passed, _ = lax.optimization_barrier((arrived, after))
        gathered += [arrived, lax.ppermute(passed, "pool", swap)]
    return gathered


def local(
    queries, span_kv, prefix_pool, hit_blocks, prefix_len, dest_blocks, out_w, residual, norm_gain
):
    tp_count = lax.axis_size("tp")
    tp_index = lax.axis_index("tp")
    pool_count = lax.axis_size("pool")
    pool_index = lax.axis_index("pool")
    prompts, rows_dev = queries.shape[:2]
    heads_dev = queries.shape[2] // HD
    kv_dev = max(1, heads_dev // (QH // KVH))
    slots_dev, block_rows = prefix_pool.shape[:2]
    d_dev = residual.shape[2]

    counts, needed, sends = prepare(
        tp_count, pool_count, heads_dev, kv_dev, hit_blocks, prefix_len, prefix_pool
    )
    span_own, own_rows = span_parts(heads_dev, kv_dev, block_rows, span_kv)
    order = sorted(range(1, tp_count), key=lambda s: -min(s, tp_count - s))
    chunks = [[over_pool(sends[0], pool_count)]]
    span = over_pool(span_own, pool_count)
    along, across = None, [chunks[0][0][2]]
    for at, shift in enumerate(order):
        pairs = [(i, (i + shift) % tp_count) for i in range(tp_count)]
        block = sends[shift]
        if at > 0:
            block, _ = lax.optimization_barrier((block, (along, across[at - 1])))
        along = lax.ppermute(block, "tp", pairs)
        passed, _ = lax.optimization_barrier((along, across[at] if at > 0 else span[2]))
        chunks.append([over_pool(passed, pool_count)])
        across.append(chunks[-1][0][2])

    last = tp_count - 1
    down = tp_index < tp_count // 2
    outs = attend(
        tuple(range(prompts)),
        counts,
        queries,
        chunks,
        kv_dev,
        span=span,
        out_w=out_w,
        which=needed,
        width=d_dev,
    )
    attended, came = outs[:prompts], outs[prompts:]

    def right_pairs(step):
        return [(i, i + 1) for i in range(last) if step >= i + 1]

    def left_pairs(step):
        return [(i, i - 1) for i in range(1, tp_count) if step >= tp_count - i]

    def is_single(step):
        return not {i for i, _ in right_pairs(step)} & {i for i, _ in left_pairs(step)}

    def send(to_right, to_left, step):
        right, left = right_pairs(step), left_pairs(step)
        if to_right is to_left and not {t for _, t in right} & {t for _, t in left}:
            return [lax.ppermute(to_right, "tp", right + left)]
        return [lax.ppermute(to_right, "tp", right), lax.ppermute(to_left, "tp", left)]

    written = lax.all_gather(own_rows[:, None], "pool", axis=1, tiled=True)
    written = written.reshape(-1, block_rows, KVH, 2 * HD)
    targets = dest_blocks.reshape(-1)
    slot_ids = pool_index * slots_dev + jnp.arange(slots_dev)
    matching = (targets[None, :] == slot_ids[:, None]).astype(jnp.int32)
    present = jnp.sum(matching, axis=1) > 0
    source = jnp.sum(matching * jnp.arange(targets.shape[0])[None, :], axis=1)
    new_pool = jnp.where(
        present[:, None, None, None], jnp.take(written, source, axis=0), prefix_pool
    )

    partials = project(needed, 1, attended, out_w, d_dev)
    begun, came = came, [send(block, block, 1) for block in came]
    for step in range(2, tp_count):
        main, other = step - 2, tp_count - step - 2
        for prompt in range(prompts):
            if step == tp_count - 1 and prompt == 0:
                came[0], new_pool = lax.optimization_barrier((came[0], new_pool))
            if is_single(step):
                block = add(jnp.int32(main), partials, prompt, came[prompt])
                came[prompt] = send(block, block, step)
                continue
            to_right, to_left = [
                add(
                    jnp.where(ours, main, other).astype(jnp.int32),
                    partials,
                    prompt,
                    [arrived],
                    begun[prompt] if other < 0 else None,
                )
                for ours, arrived in zip((down, ~down), came[prompt])
            ]
            came[prompt] = send(to_right, to_left, step)

    hidden = jnp.stack(
        [
            (
                partials[tp_count - 2, prompt * rows_dev : (prompt + 1) * rows_dev].astype(jnp.float32)
                + came[prompt][0].astype(jnp.float32)
                + came[prompt][1].astype(jnp.float32)
                + residual[prompt].astype(jnp.float32)
            ).astype(jnp.bfloat16)
            for prompt in range(prompts)
        ]
    )
    hidden = lax.optimization_barrier(hidden)
    widened = hidden.astype(jnp.float32)
    squares = jnp.sum(widened * widened, axis=2)
    total = squares
    for shift in range(1, tp_count):
        pairs = [(i, (i + shift) % tp_count) for i in range(tp_count)]
        total = total + lax.ppermute(squares, "tp", pairs)
    mean_square = total / (d_dev * tp_count)
    normed = (
        widened
        * lax.rsqrt(mean_square + epsilon)[..., None]
        * norm_gain.astype(jnp.float32)[None, None, :]
    ).astype(jnp.bfloat16)
    return hidden, normed, new_pool


def solution(mesh):
    placed = (
        P("groups", "pool", "tp"),
        P("groups", "pool", None, None),
        P(("groups", "pool"), "tp", None, None),
        P("groups", None),
        P("groups"),
        P("groups", None),
        P("tp", None),
        P("groups", "pool", "tp"),
        P("tp"),
    )
    return jax.shard_map(
        local,
        mesh=mesh,
        in_specs=placed,
        out_specs=(
            P("groups", "pool", "tp"),
            P("groups", "pool", "tp"),
            P(("groups", "pool"), "tp", None, None),
        ),
        check_vma=False,
    )
```
